32 devices in a mesh: groups: 2 (over x), ctx: 8 (over z, y), head: 2 (over core).
Axes of the slice: x: 2, y: 2, z: 4, core: 2. Of those that a mesh axis runs over, the one named last changes fastest.
Arguments:
- queries: bfloat16 [256, 4096], P(('groups', 'ctx'), 'head'), parts along dimension 0, may hold values from -150 to 150
- cache_keys: bfloat16 [32768, 2048], P(('groups', 'ctx'), 'head'), parts along dimension 0, may hold values from -5 to 5
- cache_values: bfloat16 [32768, 2048], P(('groups', 'ctx'), 'head'), parts along dimension 0, may hold values from -6 to 6
- out_weight: bfloat16 [4096, 5376], P('head', 'ctx'), may hold values from -0.1875 to 0.1875
- norm_gain: float32 [5376], P('ctx'), may hold values from 0.1 to 1.9
Outputs:
- layer_output: bfloat16 [256, 5376], P(('groups', 'head'), 'ctx'), parts along dimension 0
The draws below stay inside these ranges and needn't reach their ends.
There are 2 independent parts, one for each index of `groups`. The reference program is written for one: setup_inputs(seed, part) draws one part's arguments, and reference() takes and returns one part's arrays. A program takes and returns all parts, laid end to end along the dimension named above; an argument that names none is the same for every part. Nothing has to cross between parts.
All inputs are finite; a program needn't handle non-finite values.
Results may differ from the reference program's by a relative error of at most 0.0064.
Values may be sent and summed in bfloat16 or wider, within the bound.
A program may use at most 64 MiB of HBM per device.

```python
import jax
import jax.numpy as jnp
from jax import lax

D = 5376
HEADS = 32
KV_HEADS = 16
HEAD_DIM = 128
KEYS_DEV = 2048
Q_TOK = 128
KEYS = 16384
N_CTX = 8


def draw_pair(key):
    key_values = jax.random.truncated_normal(jax.random.fold_in(key, 11), -5.0, 5.0, (KEYS, KV_HEADS * HEAD_DIM), jnp.float32)
    query_values = jax.random.truncated_normal(jax.random.fold_in(key, 12), -5.0, 5.0, (Q_TOK, HEADS * HEAD_DIM), jnp.float32)
    return (query_values, key_values)


def draw_queries(key, part):
    return draw_pair(key)[0].astype(jnp.bfloat16)


def draw_cache_keys(key, part):
    return draw_pair(key)[1].astype(jnp.bfloat16)


def draw_out_weight(key, part):
    fan_scale = (HEADS * HEAD_DIM) ** (-0.5)
    column_pos = jnp.arange(D, dtype=jnp.float32) / max(D - 1, 1)
    base_values = jax.random.truncated_normal(key, -4.0, 4.0, (HEADS * HEAD_DIM, D), jnp.float32)
    column_scale = 1.0 + 2.0 * column_pos
    return (base_values * column_scale[None, :] * fan_scale).astype(jnp.bfloat16)


def block_scale(rng, shape, split, least, high):
    def one(axis_at, blocks):
        heights = jax.random.uniform(jax.random.fold_in(jax.random.fold_in(rng, 6), axis_at), (blocks,), jnp.float32, least / len(split), high / len(split))
        return jnp.repeat(jnp.exp(heights), shape[axis_at] // blocks).reshape((-1,) + (1,) * (len(shape) - axis_at - 1))

    loudness = one(*split[0])
    for cut in split[1:]:
        loudness = loudness * one(*cut)
    return loudness


def noise(rng, shape, spread, bound, split=(), held_as=jnp.bfloat16):
    drawn = spread * jax.random.normal(rng, shape, jnp.float32)
    if split:
        drawn = drawn * block_scale(rng, shape, split, -0.22, 0.18)
    return jnp.clip(drawn, -bound, bound).astype(held_as)


def setup_inputs(seed: int = 0, part: int = 0) -> dict:
    keys = jax.random.split(jax.random.key(seed), 6)
    own_keys = jax.random.split(jax.random.fold_in(keys[5], part), 6)
    queries = draw_queries(jax.random.fold_in(jax.random.fold_in(keys[5], part), 71), part)
    cache_keys = draw_cache_keys(jax.random.fold_in(jax.random.fold_in(keys[5], part), 71), part)
    cache_values = noise(own_keys[2], (KEYS, KV_HEADS * HEAD_DIM), 1.0, 6.0, ((0, 8), (1, 2)))
    out_weight = draw_out_weight(jax.random.fold_in(keys[5], 71), part)
    norm_gain = jnp.clip(1.0 + 0.18 * jax.random.normal(keys[4], (D,), jnp.float32), 0.1, 1.9)
    return {"queries": queries, "cache_keys": cache_keys, "cache_values": cache_values, "out_weight": out_weight, "norm_gain": norm_gain}


EPSILON = 1e-06

def attend(query_block, key_shard, value_shard):
    row_count = query_block.shape[0]
    group_size = HEADS // KV_HEADS
    head_width = group_size * HEAD_DIM
    softmax_scale = (D // HEADS) ** (-0.5)
    pair_count = key_shard.shape[1] // HEAD_DIM

    def one_head(head_index):
        query_part = lax.dynamic_slice_in_dim(query_block, head_index * head_width, head_width, 1)
        query_part = query_part.reshape(row_count, group_size, HEAD_DIM).astype(jnp.float32)
        key_part = lax.dynamic_slice_in_dim(key_shard, head_index * HEAD_DIM, HEAD_DIM, 1).astype(jnp.float32)
        value_part = lax.dynamic_slice_in_dim(value_shard, head_index * HEAD_DIM, HEAD_DIM, 1).astype(jnp.float32)
        scores = jnp.einsum('rgd,kd->grk', query_part, key_part) * softmax_scale
        maxima = lax.optimization_barrier(jnp.max(scores, axis=-1))
        expo = jnp.exp(scores - maxima[..., None])
        totals = lax.optimization_barrier(jnp.sum(expo, axis=-1))
        probabilities = expo.astype(jnp.bfloat16).astype(jnp.float32)
        weighted = jnp.einsum('grk,kd->rgd', probabilities, value_part) / totals.T[:, :, None]
        return (weighted.astype(jnp.bfloat16).reshape(row_count, head_width), (maxima + jnp.log(totals)).T)
    outputs, log_totals = lax.map(one_head, jnp.arange(pair_count, dtype=jnp.int32))
    outputs = jnp.transpose(outputs, (1, 0, 2)).reshape(row_count, -1)
    log_totals = jnp.transpose(log_totals, (1, 0, 2)).reshape(row_count, -1)
    return (outputs, log_totals)

def reference(queries, cache_keys, cache_values, out_weight, norm_gain):
    token_count = queries.shape[0]
    head_count = queries.shape[1] // HEAD_DIM

    def shard_step(state, shard_index):
        accum, running = state
        key_shard = lax.dynamic_slice_in_dim(cache_keys, shard_index * KEYS_DEV, KEYS_DEV, 0)
        value_shard = lax.dynamic_slice_in_dim(cache_values, shard_index * KEYS_DEV, KEYS_DEV, 0)
        partial_value, log_total = attend(queries, key_shard, value_shard)
        merged = jnp.logaddexp(running, log_total)
        partial_value = partial_value.reshape(token_count, head_count, HEAD_DIM).astype(jnp.float32)
        accum = accum * jnp.exp(running - merged)[:, :, None] + partial_value * jnp.exp(log_total - merged)[:, :, None]
        return ((accum, merged), None)
    start_accum = jnp.zeros((token_count, head_count, HEAD_DIM), jnp.float32)
    start_running = jnp.full((token_count, head_count), -jnp.inf, jnp.float32)
    (accum, running), unused = lax.scan(shard_step, (start_accum, start_running), jnp.arange(N_CTX, dtype=jnp.int32))
    attention = accum.reshape(token_count, -1).astype(jnp.bfloat16)
    projected = jnp.dot(attention, out_weight, preferred_element_type=jnp.float32)
    mean_square = lax.optimization_barrier(jnp.mean(projected * projected, axis=1, keepdims=True))
    normed = projected * lax.rsqrt(mean_square + EPSILON) * norm_gain.astype(jnp.float32)
    return normed.astype(jnp.bfloat16)
```

```python
import functools
import math

import jax
import jax.numpy as jnp
from jax import lax
from jax.experimental import pallas as pl
from jax.experimental.pallas import tpu as pltpu
from jax.sharding import PartitionSpec as P

HEAD_DIM = 128
GROUP = 2
EPSILON = 1e-06
KV_PER_CHUNK = 2
F32 = jnp.float32
BF16 = jnp.bfloat16
MESH = pl.DeviceIdType.MESH


def each(low, high, body):
    if high - low <= 8:
        for i in range(low, high):
            body(i)
    else:
        lax.fori_loop(low, high, lambda i, x: (body(i), x)[1], 0)


def kernel(
    n, rows, scale, model_width,
    q_ref, k_hbm, v_hbm, w_hbm, gain_ref, out_ref,
    k_buf, v_buf, w_buf, q_all, part, arrived, lse_all, merged, proj, from_head, squares,
    k_sem, v_sem, w_sem, own_sem, q_send, q_fwd, q_recv, p_send, p_recv, l_send, l_recv,
    m_send, m_fwd, m_recv, h_send, h_recv, s_send, s_recv,
):
    chunks, tokens, chunk_width = q_all.shape
    kv_heads = k_buf.shape[0]
    chunk_heads = chunk_width // HEAD_DIM
    half = n // 2
    me = lax.axis_index("ctx")
    core = lax.axis_index("head")
    across = lax.rem(me, 2)
    along = me // 2
    partner = me + 1 - 2 * across

    def peer(k):
        return lax.rem(along + k, half) * 2 + across

    def other(k):
        return lax.rem(me + k, n)

    def block(i):
        return pl.ds(pl.multiple_of(i * rows, rows), rows)

    def lanes(j):
        return pl.ds(pl.multiple_of(j * HEAD_DIM, HEAD_DIM), HEAD_DIM)

    def k_copy(j):
        return pltpu.make_async_copy(k_hbm.at[:, lanes(j)], k_buf.at[j], k_sem.at[j])

    def v_copy(j):
        return pltpu.make_async_copy(v_hbm.at[:, lanes(j)], v_buf.at[j], v_sem.at[j])

    def w_copy(c):
        return pltpu.make_async_copy(
            w_hbm.at[pl.ds(pl.multiple_of(c * chunk_width, chunk_width), chunk_width), :],
            w_buf.at[c], w_sem.at[c])

    def own_copy(c):
        return pltpu.make_async_copy(
            q_ref.at[:, pl.ds(c * chunk_width, chunk_width)], q_all.at[c, block(me), :], own_sem.at[c])

    def q_copy(c, dest):
        return pltpu.make_async_remote_copy(
            src_ref=q_ref.at[:, pl.ds(c * chunk_width, chunk_width)],
            dst_ref=q_all.at[c, block(me), :],
            send_sem=q_send.at[c, dest], recv_sem=q_recv.at[c, me],
            device_id={"ctx": dest}, device_id_type=MESH)

    def gathered(ref, send, recv, c, source, dest):
        return pltpu.make_async_remote_copy(
            src_ref=ref.at[c, block(source), :], dst_ref=ref.at[c, block(source), :],
            send_sem=send.at[c, source], recv_sem=recv.at[c, source],
            device_id={"ctx": dest}, device_id_type=MESH)

    def m_copy(c, dest):
        return pltpu.make_async_remote_copy(
            src_ref=merged.at[c, block(me), :], dst_ref=merged.at[c, block(me), :],
            send_sem=m_send.at[c, dest], recv_sem=m_recv.at[c, me],
            device_id={"ctx": dest}, device_id_type=MESH)

    def p_copy(c, dest, source):
        return pltpu.make_async_remote_copy(
            src_ref=part.at[c, block(dest), :], dst_ref=arrived.at[c, source],
            send_sem=p_send.at[c, dest], recv_sem=p_recv.at[c, source],
            device_id={"ctx": dest}, device_id_type=MESH)

    def l_copy(c, dest, source):
        return pltpu.make_async_remote_copy(
            src_ref=lse_all.at[c, source], dst_ref=lse_all.at[c, source],
            send_sem=l_send.at[c, dest], recv_sem=l_recv.at[c, source],
            device_id={"ctx": dest}, device_id_type=MESH)

    def s_copy(dest, source):
        return pltpu.make_async_remote_copy(
            src_ref=squares.at[source], dst_ref=squares.at[source],
            send_sem=s_send.at[dest], recv_sem=s_recv.at[source],
            device_id={"ctx": dest}, device_id_type=MESH)

    barrier = pltpu.get_barrier_semaphore()
    each(1, n, lambda k: pl.semaphore_signal(
        barrier, inc=1, device_id={"ctx": other(k)}, device_id_type=MESH))
    pl.semaphore_signal(barrier, inc=1, device_id={"head": 1 - core}, device_id_type=MESH)
    for c in range(chunks):
        own_copy(c).start()
    for j in range(kv_heads):
        k_copy(j).start()
        v_copy(j).start()
    for c in range(chunks):
        w_copy(c).start()
    pl.semaphore_wait(barrier, n)

    def send_q(c):
        each(1, half, lambda k: q_copy(c, peer(k)).start())
        q_copy(c, partner).start()

    for c in range(chunks):
        send_q(c)

    def forward_q(c):
        def one(k):
            copy = gathered(q_all, q_fwd, q_recv, c, peer(half - k), partner)
            copy.wait_recv()
            copy.start()
        each(1, half, one)

    def wait_q(c):
        pltpu.make_async_copy(
            q_ref.at[:, pl.ds(0, chunk_width)], q_all.at[c, block(me), :], own_sem.at[c]).wait()
        def one(k):
            source = lax.rem(partner // 2 + k, half) * 2 + lax.rem(partner, 2)
            gathered(q_all, q_fwd, q_recv, c, source, partner).wait_recv()
        each(0, half, one)

    forward_q(0)
    proj[...] = jnp.zeros_like(proj)

    exponent = scale * math.log2(math.e)
    tile = min(tokens, 128)

    def attend(c):
        wait_q(c)
        for jj in range(KV_PER_CHUNK):
            j = c * KV_PER_CHUNK + jj
            k_copy(j).wait()
            v_copy(j).wait()
            def one(t, jj=jj, j=j):
                at = pl.ds(pl.multiple_of(t * tile, tile), tile)
                queries = jnp.concatenate(
                    [q_all[c, at, (jj * GROUP + g) * HEAD_DIM:(jj * GROUP + g + 1) * HEAD_DIM]
                     for g in range(GROUP)], axis=0)
                scores = lax.dot_general(
                    queries, k_buf[j], (((1,), (1,)), ((), ())), preferred_element_type=F32)
                maxima = jnp.max(scores, axis=1, keepdims=True)
                expo = jnp.exp2((scores - maxima) * exponent)
                totals = jnp.sum(expo, axis=1, keepdims=True)
                weighted = jnp.dot(expo.astype(BF16), v_buf[j], preferred_element_type=F32) / totals
                lse = maxima * scale + jnp.log(totals)
                weighted = weighted.astype(BF16)
                diagonal = (lax.broadcasted_iota(jnp.int32, (tile, tile), 0)
                            == lax.broadcasted_iota(jnp.int32, (tile, tile), 1))
                for g in range(GROUP):
                    r = jj * GROUP + g
                    part[c, at, r * HEAD_DIM:(r + 1) * HEAD_DIM] = weighted[g * tile:(g + 1) * tile]
                    row = jnp.sum(
                        jnp.where(diagonal, lse[g * tile:(g + 1) * tile], 0.0), axis=0, keepdims=True)
                    lse_all[c, me, r:r + 1, at] = row
            each(0, tokens // tile, one)
            if jj == 0:
                @pl.when(c + 1 < chunks)
                def _():
                    forward_q(c + 1)

        def send(k):
            dest = other(k)
            l_copy(c, dest, me).start()
            p_copy(c, dest, me).start()
        each(1, n, send)

    def merge(c):
        def arrive(k):
            source = other(k)
            l_copy(c, me, source).wait_recv()
            p_copy(c, me, source).wait_recv()
        each(1, n, arrive)
        lse = lse_all[c]
        peak = jnp.max(lse, axis=0)
        whole = peak + jnp.log(jnp.sum(jnp.exp(lse - peak[None]), axis=0))
        mine = (lax.broadcasted_iota(jnp.int32, (rows, tokens), 1)
                == me * rows + lax.broadcasted_iota(jnp.int32, (rows, tokens), 0))
        total = [None] * chunk_heads
        for k in range(n):
            source = other(k)
            weight = jnp.exp(lse_all[c, source] - whole)
            values = part[c, block(me), :] if k == 0 else arrived[c, source]
            for h in range(chunk_heads):
                column = jnp.sum(jnp.where(mine, weight[h:h + 1], 0.0), axis=1, keepdims=True)
                term = values[:, h * HEAD_DIM:(h + 1) * HEAD_DIM].astype(F32) * column
                total[h] = term if k == 0 else total[h] + term
        for h in range(chunk_heads):
            merged[c, block(me), h * HEAD_DIM:(h + 1) * HEAD_DIM] = total[h].astype(BF16)
        each(1, half, lambda k: m_copy(c, peer(k)).start())
        m_copy(c, partner).start()

    def forward_m(c):
        def one(k):
            copy = gathered(merged, m_fwd, m_recv, c, peer(half - k), partner)
            copy.wait_recv()
            copy.start()
        each(1, half, one)

    def project(c):
        def one(k):
            source = lax.rem(partner // 2 + k, half) * 2 + lax.rem(partner, 2)
            gathered(merged, m_fwd, m_recv, c, source, partner).wait_recv()
        each(0, half, one)
        w_copy(c).wait()
        proj[...] += jnp.dot(merged[c], w_buf[c], preferred_element_type=F32)

    def step(t, carry):
        @pl.when(t < chunks)
        def _():
            attend(t)

        @pl.when((t >= 1) & (t <= chunks))
        def _():
            merge(t - 1)

        @pl.when((t >= 2) & (t <= chunks + 1))
        def _():
            forward_m(t - 2)

        @pl.when(t >= 3)
        def _():
            project(t - 3)
        return carry

    lax.fori_loop(0, chunks + 3, step, 0)

    split = tokens // 2
    def rows_of(i):
        return pl.ds(pl.multiple_of(i * split, split), split)
    exchange = pltpu.make_async_remote_copy(
        src_ref=proj.at[rows_of(1 - core), :], dst_ref=from_head, send_sem=h_send, recv_sem=h_recv,
        device_id={"head": 1 - core}, device_id_type=MESH)
    exchange.start()
    exchange.wait()
    summed = proj[rows_of(core), :] + from_head[...]
    square = jnp.sum(summed * summed, axis=1, keepdims=True)
    diagonal = (lax.broadcasted_iota(jnp.int32, (split, split), 0)
                == lax.broadcasted_iota(jnp.int32, (split, split), 1))
    squares[me] = jnp.broadcast_to(
        jnp.sum(jnp.where(diagonal, square, 0.0), axis=0, keepdims=True), (8, split))
    each(1, n, lambda k: s_copy(other(k), me).start())
    each(1, n, lambda k: s_copy(me, other(k)).wait_recv())
    square_row = jnp.sum(squares[...], axis=0)[0:1]
    square_sums = jnp.sum(jnp.where(diagonal, square_row, 0.0), axis=1, keepdims=True)
    normed = summed * lax.rsqrt(square_sums / model_width + EPSILON) * gain_ref[...]
    out_ref[...] = normed.astype(BF16)

    def drain(c, carry):
        def sent_gather(k):
            gathered(q_all, q_send, q_recv, c, peer(k), partner).wait_send()
            gathered(q_all, q_fwd, q_recv, c, peer(k), partner).wait_send()
            m_copy(c, peer(k)).wait_send()
            gathered(merged, m_fwd, m_recv, c, peer(k), partner).wait_send()
        each(1, half, sent_gather)
        gathered(q_all, q_send, q_recv, c, partner, partner).wait_send()
        m_copy(c, partner).wait_send()
        def sent_part(k):
            l_copy(c, other(k), me).wait_send()
            p_copy(c, other(k), me).wait_send()
        each(1, n, sent_part)
        return carry
    lax.fori_loop(0, chunks, drain, 0)
    each(1, n, lambda k: s_copy(other(k), me).wait_send())


def local(model_heads, queries, cache_keys, cache_values, out_weight, norm_gain):
    n = lax.axis_size("ctx")
    rows, width = queries.shape
    keys, kv_width = cache_keys.shape
    kv_heads = kv_width // HEAD_DIM
    columns = out_weight.shape[1]
    tokens = rows * n
    model_width = columns * n
    chunks = kv_heads // KV_PER_CHUNK
    chunk_width = width // chunks
    scale = float(model_width // model_heads) ** (-0.5)
    dma = pltpu.SemaphoreType.DMA
    any_space = pl.BlockSpec(memory_space=pl.ANY)
    vmem = pl.BlockSpec(memory_space=pltpu.VMEM)
    return pl.pallas_call(
        functools.partial(kernel, n, rows, scale, model_width),
        out_shape=jax.ShapeDtypeStruct((tokens // 2, columns), BF16),
        in_specs=[vmem, any_space, any_space, any_space, vmem],
        out_specs=vmem,
        scratch_shapes=[
            pltpu.VMEM((kv_heads, keys, HEAD_DIM), BF16),
            pltpu.VMEM((kv_heads, keys, HEAD_DIM), BF16),
            pltpu.VMEM((chunks, chunk_width, columns), BF16),
            pltpu.VMEM((chunks, tokens, chunk_width), BF16),
            pltpu.VMEM((chunks, tokens, chunk_width), BF16),
            pltpu.VMEM((chunks, n, rows, chunk_width), BF16),
            pltpu.VMEM((chunks, n, chunk_width // HEAD_DIM, tokens), F32),
            pltpu.VMEM((chunks, tokens, chunk_width), BF16),
            pltpu.VMEM((tokens, columns), F32),
            pltpu.VMEM((tokens // 2, columns), F32),
            pltpu.VMEM((n, 8, tokens // 2), F32),
            dma((kv_heads,)), dma((kv_heads,)), dma((chunks,)), dma((chunks,)),
            dma((chunks, n)), dma((chunks, n)), dma((chunks, n)),
            dma((chunks, n)), dma((chunks, n)), dma((chunks, n)), dma((chunks, n)),
            dma((chunks, n)), dma((chunks, n)), dma((chunks, n)),
            dma, dma, dma((n,)), dma((n,)),
        ],
        compiler_params=pltpu.CompilerParams(
            collective_id=0, has_side_effects=True, vmem_limit_bytes=56 * 1024 * 1024),
    )(queries, cache_keys, cache_values, out_weight, norm_gain[None, :])


def solution(mesh):
    in_specs = (
        P(("groups", "ctx"), "head"),
        P(("groups", "ctx"), "head"),
        P(("groups", "ctx"), "head"),
        P("head", "ctx"),
        P("ctx"),
    )
    out_specs = P(("groups", "head"), "ctx")

    def whole(queries, *rest):
        body = functools.partial(local, queries.shape[1] // HEAD_DIM)
        return jax.shard_map(
            body, mesh=mesh, in_specs=in_specs, out_specs=out_specs, check_vma=False)(queries, *rest)
    return whole
```

```python
import functools
import math

import jax
import jax.numpy as jnp
from jax import lax
from jax.experimental import pallas as pl
from jax.experimental.pallas import tpu as pltpu
from jax.sharding import PartitionSpec as P

HEAD_DIM = 128
GROUP = 2
EPSILON = 1e-06
KV_PER_CHUNK = 4
F32 = jnp.float32
BF16 = jnp.bfloat16
MESH = pl.DeviceIdType.MESH


def each(low, high, body):
    if high - low <= 8:
        for i in range(low, high):
            body(i)
    else:
        lax.fori_loop(low, high, lambda i, x: (body(i), x)[1], 0)


def kernel(
    n, rows, scale, model_width,
    q_ref, k_hbm, v_hbm, w_hbm, out_ref,
    k_buf, v_buf, w_buf, q_all, part, arrived, lse_all, merged, proj, from_head, squares,
    k_sem, v_sem, w_sem, own_sem, q_send, q_fwd, q_recv, p_send, p_recv, l_send, l_recv,
    m_send, m_fwd, m_recv, h_send, h_recv, s_send, s_recv,
):
    chunks, tokens, chunk_width = q_all.shape
    kv_heads = k_buf.shape[0]
    chunk_heads = chunk_width // HEAD_DIM
    half = n // 2
    me = lax.axis_index("ctx")
    core = lax.axis_index("head")
    across = lax.rem(me, 2)
    along = me // 2
    partner = me + 1 - 2 * across

    def peer(k):
        return lax.rem(along + k, half) * 2 + across

    def other(k):
        return lax.rem(me + k, n)

    def block(i):
        return pl.ds(pl.multiple_of(i * rows, rows), rows)

    def lanes(j):
        return pl.ds(pl.multiple_of(j * HEAD_DIM, HEAD_DIM), HEAD_DIM)

    def k_copy(j):
        return pltpu.make_async_copy(k_hbm.at[:, lanes(j)], k_buf.at[j], k_sem.at[j])

    def v_copy(j):
        return pltpu.make_async_copy(v_hbm.at[:, lanes(j)], v_buf.at[j], v_sem.at[j])

    def w_copy(c):
        return pltpu.make_async_copy(
            w_hbm.at[:, pl.ds(pl.multiple_of(c * chunk_width, chunk_width), chunk_width)],
            w_buf.at[c], w_sem.at[c])

    def own_copy(c):
        return pltpu.make_async_copy(
            q_ref.at[:, pl.ds(c * chunk_width, chunk_width)], q_all.at[c, block(me), :], own_sem.at[c])

    def q_copy(c, dest):
        return pltpu.make_async_remote_copy(
            src_ref=q_ref.at[:, pl.ds(c * chunk_width, chunk_width)],
            dst_ref=q_all.at[c, block(me), :],
            send_sem=q_send.at[c, dest], recv_sem=q_recv.at[c, me],
            device_id={"ctx": dest}, device_id_type=MESH)

    def gathered(ref, send, recv, c, source, dest):
        return pltpu.make_async_remote_copy(
            src_ref=ref.at[c, block(source), :], dst_ref=ref.at[c, block(source), :],
            send_sem=send.at[c, source], recv_sem=recv.at[c, source],
            device_id={"ctx": dest}, device_id_type=MESH)

    def m_copy(c, dest):
        return pltpu.make_async_remote_copy(
            src_ref=merged.at[c, block(me), :], dst_ref=merged.at[c, block(me), :],
            send_sem=m_send.at[c, dest], recv_sem=m_recv.at[c, me],
            device_id={"ctx": dest}, device_id_type=MESH)

    def p_copy(c, dest, source):
        return pltpu.make_async_remote_copy(
            src_ref=part.at[c, block(dest), :], dst_ref=arrived.at[c, source],
            send_sem=p_send.at[c, dest], recv_sem=p_recv.at[c, source],
            device_id={"ctx": dest}, device_id_type=MESH)

    def l_copy(c, dest, source):
        return pltpu.make_async_remote_copy(
            src_ref=lse_all.at[c, source], dst_ref=lse_all.at[c, source],
            send_sem=l_send.at[c, dest], recv_sem=l_recv.at[c, source],
            device_id={"ctx": dest}, device_id_type=MESH)

    def s_copy(dest, source):
        return pltpu.make_async_remote_copy(
            src_ref=squares.at[source], dst_ref=squares.at[source],
            send_sem=s_send.at[dest], recv_sem=s_recv.at[source],
            device_id={"ctx": dest}, device_id_type=MESH)

    barrier = pltpu.get_barrier_semaphore()
    each(1, n, lambda k: pl.semaphore_signal(
        barrier, inc=1, device_id={"ctx": other(k)}, device_id_type=MESH))
    pl.semaphore_signal(barrier, inc=1, device_id={"head": 1 - core}, device_id_type=MESH)
    for c in range(chunks):
        own_copy(c).start()
    for j in range(kv_heads):
        k_copy(j).start()
        v_copy(j).start()
    for c in range(chunks):
        w_copy(c).start()
    pl.semaphore_wait(barrier, n)

    def send_q(c):
        each(1, half, lambda k: q_copy(c, peer(k)).start())
        q_copy(c, partner).start()

    for c in range(chunks):
        send_q(c)

    def forward_q(c):
        def one(k):
            copy = gathered(q_all, q_fwd, q_recv, c, peer(half - k), partner)
            copy.wait_recv()
            copy.start()
        each(1, half, one)

    def wait_q(c):
        pltpu.make_async_copy(
            q_ref.at[:, pl.ds(0, chunk_width)], q_all.at[c, block(me), :], own_sem.at[c]).wait()
        def one(k):
            source = lax.rem(partner // 2 + k, half) * 2 + lax.rem(partner, 2)
            gathered(q_all, q_fwd, q_recv, c, source, partner).wait_recv()
        each(0, half, one)

    forward_q(0)
    proj[...] = jnp.zeros_like(proj)

    exponent = scale * math.log2(math.e)
    tile = min(tokens, 128)

    def attend(c):
        wait_q(c)
        for jj in range(KV_PER_CHUNK):
            j = c * KV_PER_CHUNK + jj
            k_copy(j).wait()
            v_copy(j).wait()
            def one(t, jj=jj, j=j):
                at = pl.ds(pl.multiple_of(t * tile, tile), tile)
                queries = jnp.concatenate(
                    [q_all[c, at, (jj * GROUP + g) * HEAD_DIM:(jj * GROUP + g + 1) * HEAD_DIM]
                     for g in range(GROUP)], axis=0)
                scores = lax.dot_general(
                    queries, k_buf[j], (((1,), (1,)), ((), ())), preferred_element_type=F32)
                maxima = jnp.max(scores, axis=1, keepdims=True)
                expo = jnp.exp2((scores - maxima) * exponent)
                totals = jnp.sum(expo, axis=1, keepdims=True)
                weighted = jnp.dot(expo.astype(BF16), v_buf[j], preferred_element_type=F32) / totals
                lse = maxima * scale + jnp.log(totals)
                weighted = weighted.astype(BF16)
                diagonal = (lax.broadcasted_iota(jnp.int32, (tile, tile), 0)
                            == lax.broadcasted_iota(jnp.int32, (tile, tile), 1))
                for g in range(GROUP):
                    r = jj * GROUP + g
                    part[c, at, r * HEAD_DIM:(r + 1) * HEAD_DIM] = weighted[g * tile:(g + 1) * tile]
                    row = jnp.sum(
                        jnp.where(diagonal, lse[g * tile:(g + 1) * tile], 0.0), axis=0, keepdims=True)
                    lse_all[c, me, r:r + 1, at] = row
            each(0, tokens // tile, one)
            if jj == 0:
                @pl.when(c + 1 < chunks)
                def _():
                    forward_q(c + 1)

        def send(k):
            dest = other(k)
            l_copy(c, dest, me).start()
            p_copy(c, dest, me).start()
        each(1, n, send)

    def merge(c):
        def arrive(k):
            source = other(k)
            l_copy(c, me, source).wait_recv()
            p_copy(c, me, source).wait_recv()
        each(1, n, arrive)
        lse = lse_all[c]
        peak = jnp.max(lse, axis=0)
        whole = peak + jnp.log(jnp.sum(jnp.exp(lse - peak[None]), axis=0))
        mine = (lax.broadcasted_iota(jnp.int32, (rows, tokens), 1)
                == me * rows + lax.broadcasted_iota(jnp.int32, (rows, tokens), 0))
        total = [None] * chunk_heads
        for k in range(n):
            source = other(k)
            weight = jnp.exp(lse_all[c, source] - whole)
            values = part[c, block(me), :] if k == 0 else arrived[c, source]
            for h in range(chunk_heads):
                column = jnp.sum(jnp.where(mine, weight[h:h + 1], 0.0), axis=1, keepdims=True)
                term = values[:, h * HEAD_DIM:(h + 1) * HEAD_DIM].astype(F32) * column
                total[h] = term if k == 0 else total[h] + term
        for h in range(chunk_heads):
            merged[c, block(me), h * HEAD_DIM:(h + 1) * HEAD_DIM] = total[h].astype(BF16)
        each(1, half, lambda k: m_copy(c, peer(k)).start())
        m_copy(c, partner).start()

    def forward_m(c):
        def one(k):
            copy = gathered(merged, m_fwd, m_recv, c, peer(half - k), partner)
            copy.wait_recv()
            copy.start()
        each(1, half, one)

    def project(c):
        def one(k):
            source = lax.rem(partner // 2 + k, half) * 2 + lax.rem(partner, 2)
            gathered(merged, m_fwd, m_recv, c, source, partner).wait_recv()
        each(0, half, one)
        w_copy(c).wait()
        proj[...] += lax.dot_general(
            merged[c], w_buf[c], (((1,), (1,)), ((), ())), preferred_element_type=F32)

    def step(t, carry):
        @pl.when(t < chunks)
        def _():
            attend(t)

        @pl.when((t >= 1) & (t <= chunks))
        def _():
            merge(t - 1)

        @pl.when((t >= 2) & (t <= chunks + 1))
        def _():
            forward_m(t - 2)

        @pl.when(t >= 3)
        def _():
            project(t - 3)
        return carry

    lax.fori_loop(0, chunks + 3, step, 0)

    split = tokens // 2
    def rows_of(i):
        return pl.ds(pl.multiple_of(i * split, split), split)
    exchange = pltpu.make_async_remote_copy(
        src_ref=proj.at[rows_of(1 - core), :], dst_ref=from_head, send_sem=h_send, recv_sem=h_recv,
        device_id={"head": 1 - core}, device_id_type=MESH)
    exchange.start()
    exchange.wait()
    summed = proj[rows_of(core), :] + from_head[...]
    square = jnp.sum(summed * summed, axis=1, keepdims=True)
    diagonal = (lax.broadcasted_iota(jnp.int32, (split, split), 0)
                == lax.broadcasted_iota(jnp.int32, (split, split), 1))
    squares[me] = jnp.broadcast_to(
        jnp.sum(jnp.where(diagonal, square, 0.0), axis=0, keepdims=True), (8, split))
    each(1, n, lambda k: s_copy(other(k), me).start())
    each(1, n, lambda k: s_copy(me, other(k)).wait_recv())
    square_row = jnp.sum(squares[...], axis=0)[0:1]
    square_sums = jnp.sum(jnp.where(diagonal, square_row, 0.0), axis=1, keepdims=True)
    out_ref[...] = summed * lax.rsqrt(square_sums / model_width + EPSILON)

    def drain(c, carry):
        def sent_gather(k):
            gathered(q_all, q_send, q_recv, c, peer(k), partner).wait_send()
            gathered(q_all, q_fwd, q_recv, c, peer(k), partner).wait_send()
            m_copy(c, peer(k)).wait_send()
            gathered(merged, m_fwd, m_recv, c, peer(k), partner).wait_send()
        each(1, half, sent_gather)
        gathered(q_all, q_send, q_recv, c, partner, partner).wait_send()
        m_copy(c, partner).wait_send()
        def sent_part(k):
            l_copy(c, other(k), me).wait_send()
            p_copy(c, other(k), me).wait_send()
        each(1, n, sent_part)
        return carry
    lax.fori_loop(0, chunks, drain, 0)
    each(1, n, lambda k: s_copy(other(k), me).wait_send())


def local(model_heads, queries, cache_keys, cache_values, out_weight, norm_gain):
    n = lax.axis_size("ctx")
    rows, width = queries.shape
    keys, kv_width = cache_keys.shape
    kv_heads = kv_width // HEAD_DIM
    columns = out_weight.shape[1]
    tokens = rows * n
    model_width = columns * n
    chunks = kv_heads // KV_PER_CHUNK
    chunk_width = width // chunks
    scale = float(model_width // model_heads) ** (-0.5)
    dma = pltpu.SemaphoreType.DMA
    any_space = pl.BlockSpec(memory_space=pl.ANY)
    vmem = pl.BlockSpec(memory_space=pltpu.VMEM)
    normed = pl.pallas_call(
        functools.partial(kernel, n, rows, scale, model_width),
        out_shape=jax.ShapeDtypeStruct((tokens // 2, columns), F32),
        in_specs=[vmem, any_space, any_space, any_space],
        out_specs=vmem,
        scratch_shapes=[
            pltpu.VMEM((kv_heads, keys, HEAD_DIM), BF16),
            pltpu.VMEM((kv_heads, keys, HEAD_DIM), BF16),
            pltpu.VMEM((chunks, columns, chunk_width), BF16),
            pltpu.VMEM((chunks, tokens, chunk_width), BF16),
            pltpu.VMEM((chunks, tokens, chunk_width), BF16),
            pltpu.VMEM((chunks, n, rows, chunk_width), BF16),
            pltpu.VMEM((chunks, n, chunk_width // HEAD_DIM, tokens), F32),
            pltpu.VMEM((chunks, tokens, chunk_width), BF16),
            pltpu.VMEM((tokens, columns), F32),
            pltpu.VMEM((tokens // 2, columns), F32),
            pltpu.VMEM((n, 8, tokens // 2), F32),
            dma((kv_heads,)), dma((kv_heads,)), dma((chunks,)), dma((chunks,)),
            dma((chunks, n)), dma((chunks, n)), dma((chunks, n)),
            dma((chunks, n)), dma((chunks, n)), dma((chunks, n)), dma((chunks, n)),
            dma((chunks, n)), dma((chunks, n)), dma((chunks, n)),
            dma, dma, dma((n,)), dma((n,)),
        ],
        compiler_params=pltpu.CompilerParams(
            collective_id=0, has_side_effects=True, vmem_limit_bytes=56 * 1024 * 1024),
    )(queries, cache_keys, cache_values, out_weight.T)
    return (normed * norm_gain[None, :]).astype(BF16)


def solution(mesh):
    in_specs = (
        P(("groups", "ctx"), "head"),
        P(("groups", "ctx"), "head"),
        P(("groups", "ctx"), "head"),
        P("head", "ctx"),
        P("ctx"),
    )
    out_specs = P(("groups", "head"), "ctx")

    def whole(queries, *rest):
        body = functools.partial(local, queries.shape[1] // HEAD_DIM)
        return jax.shard_map(
            body, mesh=mesh, in_specs=in_specs, out_specs=out_specs, check_vma=False)(queries, *rest)
    return whole
```

```python
import functools
import math

import jax
import jax.numpy as jnp
from jax import lax
from jax.experimental import pallas as pl
from jax.experimental.pallas import tpu as pltpu
from jax.sharding import PartitionSpec as P

HEAD_DIM = 128
GROUP = 2
EPSILON = 1e-06
KV_PER_CHUNK = 4
KV_PER_SEND = 2
F32 = jnp.float32
BF16 = jnp.bfloat16
MESH = pl.DeviceIdType.MESH


def each(low, high, body):
    if high - low <= 8:
        for i in range(low, high):
            body(i)
    else:
        lax.fori_loop(low, high, lambda i, x: (body(i), x)[1], 0)


def kernel(
    n, rows, scale, model_width,
    q_ref, k_hbm, v_hbm, w_hbm, out_ref,
    k_buf, v_buf, w_buf, q_all, part, arrived, lse_all, merged, proj, from_head, squares,
    k_sem, v_sem, w_sem, own_sem, q_send, q_fwd, q_recv, p_send, p_recv, l_send, l_recv,
    m_send, m_fwd, m_recv, h_send, h_recv, s_send, s_recv,
):
    q_chunks, tokens, q_width = q_all.shape
    chunks, _, chunk_width = part.shape
    kv_heads = k_buf.shape[0]
    chunk_heads = chunk_width // HEAD_DIM
    half = n // 2
    me = lax.axis_index("ctx")
    core = lax.axis_index("head")
    across = lax.rem(me, 2)
    along = me // 2
    partner = me + 1 - 2 * across

    def peer(k):
        return lax.rem(along + k, half) * 2 + across

    def other(k):
        return lax.rem(me + k, n)

    def block(i):
        return pl.ds(pl.multiple_of(i * rows, rows), rows)

    def lanes(j):
        return pl.ds(pl.multiple_of(j * HEAD_DIM, HEAD_DIM), HEAD_DIM)

    def k_copy(j):
        return pltpu.make_async_copy(k_hbm.at[:, lanes(j)], k_buf.at[j], k_sem.at[j])

    def v_copy(j):
        return pltpu.make_async_copy(v_hbm.at[:, lanes(j)], v_buf.at[j], v_sem.at[j])

    def w_copy(c):
        return pltpu.make_async_copy(
            w_hbm.at[:, pl.ds(pl.multiple_of(c * chunk_width, chunk_width), chunk_width)],
            w_buf.at[c], w_sem.at[c])

    def own_copy(c):
        return pltpu.make_async_copy(
            q_ref.at[:, pl.ds(c * q_width, q_width)], q_all.at[c, block(me), :], own_sem.at[c])

    def q_copy(c, dest):
        return pltpu.make_async_remote_copy(
            src_ref=q_ref.at[:, pl.ds(c * q_width, q_width)],
            dst_ref=q_all.at[c, block(me), :],
            send_sem=q_send.at[c, dest], recv_sem=q_recv.at[c, me],
            device_id={"ctx": dest}, device_id_type=MESH)

    def gathered(ref, send, recv, c, source, dest):
        return pltpu.make_async_remote_copy(
            src_ref=ref.at[c, block(source), :], dst_ref=ref.at[c, block(source), :],
            send_sem=send.at[c, source], recv_sem=recv.at[c, source],
            device_id={"ctx": dest}, device_id_type=MESH)

    def m_copy(c, dest):
        return pltpu.make_async_remote_copy(
            src_ref=merged.at[c, block(me), :], dst_ref=merged.at[c, block(me), :],
            send_sem=m_send.at[c, dest], recv_sem=m_recv.at[c, me],
            device_id={"ctx": dest}, device_id_type=MESH)

    def p_copy(c, dest, source):
        return pltpu.make_async_remote_copy(
            src_ref=part.at[c, block(dest), :], dst_ref=arrived.at[c, source],
            send_sem=p_send.at[c, dest], recv_sem=p_recv.at[c, source],
            device_id={"ctx": dest}, device_id_type=MESH)

    def l_copy(c, dest, source):
        return pltpu.make_async_remote_copy(
            src_ref=lse_all.at[c, source], dst_ref=lse_all.at[c, source],
            send_sem=l_send.at[c, dest], recv_sem=l_recv.at[c, source],
            device_id={"ctx": dest}, device_id_type=MESH)

    def s_copy(dest, source):
        return pltpu.make_async_remote_copy(
            src_ref=squares.at[source], dst_ref=squares.at[source],
            send_sem=s_send.at[dest], recv_sem=s_recv.at[source],
            device_id={"ctx": dest}, device_id_type=MESH)

    barrier = pltpu.get_barrier_semaphore()
    each(1, n, lambda k: pl.semaphore_signal(
        barrier, inc=1, device_id={"ctx": other(k)}, device_id_type=MESH))
    pl.semaphore_signal(barrier, inc=1, device_id={"head": 1 - core}, device_id_type=MESH)
    for c in range(q_chunks):
        own_copy(c).start()
    for j in range(kv_heads):
        k_copy(j).start()
        v_copy(j).start()
    for c in range(chunks):
        w_copy(c).start()
    pl.semaphore_wait(barrier, n)

    def send_q(c):
        each(1, half, lambda k: q_copy(c, peer(k)).start())
        q_copy(c, partner).start()

    for c in range(q_chunks):
        send_q(c)

    def forward_q(c):
        def one(k):
            copy = gathered(q_all, q_fwd, q_recv, c, peer(half - k), partner)
            copy.wait_recv()
            copy.start()
        each(1, half, one)

    def wait_q(c):
        pltpu.make_async_copy(
            q_ref.at[:, pl.ds(0, q_width)], q_all.at[c, block(me), :], own_sem.at[c]).wait()
        def one(k):
            source = lax.rem(partner // 2 + k, half) * 2 + lax.rem(partner, 2)
            gathered(q_all, q_fwd, q_recv, c, source, partner).wait_recv()
        each(0, half, one)

    for c in range(min(2, q_chunks)):
        forward_q(c)
    proj[...] = jnp.zeros_like(proj)

    exponent = scale * math.log2(math.e)
    tile = min(tokens, 128)

    def attend(c):
        for jj in range(KV_PER_CHUNK):
            sent = c * (KV_PER_CHUNK // KV_PER_SEND) + jj // KV_PER_SEND
            if jj % KV_PER_SEND == 0:
                wait_q(sent)
            j = c * KV_PER_CHUNK + jj
            k_copy(j).wait()
            v_copy(j).wait()
            def one(t, jj=jj, j=j, sent=sent, lane=jj % KV_PER_SEND * GROUP):
                at = pl.ds(pl.multiple_of(t * tile, tile), tile)
                queries = jnp.concatenate(
                    [q_all[sent, at, (lane + g) * HEAD_DIM:(lane + g + 1) * HEAD_DIM]
                     for g in range(GROUP)], axis=0)
                scores = lax.dot_general(
                    queries, k_buf[j], (((1,), (1,)), ((), ())), preferred_element_type=F32)
                maxima = jnp.max(scores, axis=1, keepdims=True)
                expo = jnp.exp2((scores - maxima) * exponent)
                totals = jnp.sum(expo, axis=1, keepdims=True)
                weighted = jnp.dot(expo.astype(BF16), v_buf[j], preferred_element_type=F32) / totals
                lse = maxima * scale + jnp.log(totals)
                weighted = weighted.astype(BF16)
                diagonal = (lax.broadcasted_iota(jnp.int32, (tile, tile), 0)
                            == lax.broadcasted_iota(jnp.int32, (tile, tile), 1))
                for g in range(GROUP):
                    r = jj * GROUP + g
                    part[c, at, r * HEAD_DIM:(r + 1) * HEAD_DIM] = weighted[g * tile:(g + 1) * tile]
                    row = jnp.sum(
                        jnp.where(diagonal, lse[g * tile:(g + 1) * tile], 0.0), axis=0, keepdims=True)
                    lse_all[c, me, r:r + 1, at] = row
            each(0, tokens // tile, one)
            if jj % KV_PER_SEND == 0:
                @pl.when(sent + 2 < q_chunks)
                def _(sent=sent):
                    forward_q(sent + 2)

        def send(k):
            dest = other(k)
            l_copy(c, dest, me).start()
            p_copy(c, dest, me).start()
        each(1, n, send)

    def merge(c):
        def arrive(k):
            source = other(k)
            l_copy(c, me, source).wait_recv()
            p_copy(c, me, source).wait_recv()
        each(1, n, arrive)
        lse = lse_all[c]
        peak = jnp.max(lse, axis=0)
        whole = peak + jnp.log(jnp.sum(jnp.exp(lse - peak[None]), axis=0))
        mine = (lax.broadcasted_iota(jnp.int32, (rows, tokens), 1)
                == me * rows + lax.broadcasted_iota(jnp.int32, (rows, tokens), 0))
        total = [None] * chunk_heads
        for k in range(n):
            source = other(k)
            weight = jnp.exp(lse_all[c, source] - whole)
            values = part[c, block(me), :] if k == 0 else arrived[c, source]
            for h in range(chunk_heads):
                column = jnp.sum(jnp.where(mine, weight[h:h + 1], 0.0), axis=1, keepdims=True)
                term = values[:, h * HEAD_DIM:(h + 1) * HEAD_DIM].astype(F32) * column
                total[h] = term if k == 0 else total[h] + term
        for h in range(chunk_heads):
            merged[c, block(me), h * HEAD_DIM:(h + 1) * HEAD_DIM] = total[h].astype(BF16)
        each(1, half, lambda k: m_copy(c, peer(k)).start())
        m_copy(c, partner).start()

    def forward_m(c):
        def one(k):
            copy = gathered(merged, m_fwd, m_recv, c, peer(half - k), partner)
            copy.wait_recv()
            copy.start()
        each(1, half, one)

    def project(c):
        def one(k):
            source = lax.rem(partner // 2 + k, half) * 2 + lax.rem(partner, 2)
            gathered(merged, m_fwd, m_recv, c, source, partner).wait_recv()
        each(0, half, one)
        w_copy(c).wait()
        proj[...] += lax.dot_general(
            merged[c], w_buf[c], (((1,), (1,)), ((), ())), preferred_element_type=F32)

    def step(t, carry):
        @pl.when(t < chunks)
        def _():
            attend(t)

        @pl.when((t >= 1) & (t <= chunks))
        def _():
            merge(t - 1)

        @pl.when((t >= 2) & (t <= chunks + 1))
        def _():
            forward_m(t - 2)

        @pl.when(t >= 3)
        def _():
            project(t - 3)
        return carry

    lax.fori_loop(0, chunks + 3, step, 0)

    split = tokens // 2
    def rows_of(i):
        return pl.ds(pl.multiple_of(i * split, split), split)
    exchange = pltpu.make_async_remote_copy(
        src_ref=proj.at[rows_of(1 - core), :], dst_ref=from_head, send_sem=h_send, recv_sem=h_recv,
        device_id={"head": 1 - core}, device_id_type=MESH)
    exchange.start()
    exchange.wait()
    summed = proj[rows_of(core), :] + from_head[...]
    square = jnp.sum(summed * summed, axis=1, keepdims=True)
    diagonal = (lax.broadcasted_iota(jnp.int32, (split, split), 0)
                == lax.broadcasted_iota(jnp.int32, (split, split), 1))
    squares[me] = jnp.broadcast_to(
        jnp.sum(jnp.where(diagonal, square, 0.0), axis=0, keepdims=True), (8, split))
    each(1, n, lambda k: s_copy(other(k), me).start())
    def drain_q(c, carry):
        each(1, half, lambda k: gathered(q_all, q_send, q_recv, c, peer(k), partner).wait_send())
        each(1, half, lambda k: gathered(q_all, q_fwd, q_recv, c, peer(k), partner).wait_send())
        gathered(q_all, q_send, q_recv, c, partner, partner).wait_send()
        return carry
    lax.fori_loop(0, q_chunks, drain_q, 0)

    def drain(c, carry):
        def sent_gather(k):
            m_copy(c, peer(k)).wait_send()
            gathered(merged, m_fwd, m_recv, c, peer(k), partner).wait_send()
        each(1, half, sent_gather)
        m_copy(c, partner).wait_send()
        def sent_part(k):
            l_copy(c, other(k), me).wait_send()
            p_copy(c, other(k), me).wait_send()
        each(1, n, sent_part)
        return carry
    lax.fori_loop(0, chunks, drain, 0)
    each(1, n, lambda k: s_copy(me, other(k)).wait_recv())
    square_row = jnp.sum(squares[...], axis=0)[0:1]
    square_sums = jnp.sum(jnp.where(diagonal, square_row, 0.0), axis=1, keepdims=True)
    out_ref[...] = summed * lax.rsqrt(square_sums / model_width + EPSILON)

    each(1, n, lambda k: s_copy(other(k), me).wait_send())


def local(model_heads, queries, cache_keys, cache_values, out_weight, norm_gain):
    n = lax.axis_size("ctx")
    rows, width = queries.shape
    keys, kv_width = cache_keys.shape
    kv_heads = kv_width // HEAD_DIM
    columns = out_weight.shape[1]
    tokens = rows * n
    model_width = columns * n
    chunks = kv_heads // KV_PER_CHUNK
    chunk_width = width // chunks
    q_chunks = kv_heads // KV_PER_SEND
    scale = float(model_width // model_heads) ** (-0.5)
    dma = pltpu.SemaphoreType.DMA
    any_space = pl.BlockSpec(memory_space=pl.ANY)
    vmem = pl.BlockSpec(memory_space=pltpu.VMEM)
    normed = pl.pallas_call(
        functools.partial(kernel, n, rows, scale, model_width),
        out_shape=jax.ShapeDtypeStruct((tokens // 2, columns), F32),
        in_specs=[vmem, any_space, any_space, any_space],
        out_specs=vmem,
        scratch_shapes=[
            pltpu.VMEM((kv_heads, keys, HEAD_DIM), BF16),
            pltpu.VMEM((kv_heads, keys, HEAD_DIM), BF16),
            pltpu.VMEM((chunks, columns, chunk_width), BF16),
            pltpu.VMEM((q_chunks, tokens, width // q_chunks), BF16),
            pltpu.VMEM((chunks, tokens, chunk_width), BF16),
            pltpu.VMEM((chunks, n, rows, chunk_width), BF16),
            pltpu.VMEM((chunks, n, chunk_width // HEAD_DIM, tokens), F32),
            pltpu.VMEM((chunks, tokens, chunk_width), BF16),
            pltpu.VMEM((tokens, columns), F32),
            pltpu.VMEM((tokens // 2, columns), F32),
            pltpu.VMEM((n, 8, tokens // 2), F32),
            dma((kv_heads,)), dma((kv_heads,)), dma((chunks,)), dma((q_chunks,)),
            dma((q_chunks, n)), dma((q_chunks, n)), dma((q_chunks, n)),
            dma((chunks, n)), dma((chunks, n)), dma((chunks, n)), dma((chunks, n)),
            dma((chunks, n)), dma((chunks, n)), dma((chunks, n)),
            dma, dma, dma((n,)), dma((n,)),
        ],
        compiler_params=pltpu.CompilerParams(
            collective_id=0, has_side_effects=True, vmem_limit_bytes=56 * 1024 * 1024),
    )(queries, cache_keys, cache_values, out_weight.T)
    return (normed * norm_gain[None, :]).astype(BF16)


def solution(mesh):
    in_specs = (
        P(("groups", "ctx"), "head"),
        P(("groups", "ctx"), "head"),
        P(("groups", "ctx"), "head"),
        P("head", "ctx"),
        P("ctx"),
    )
    out_specs = P(("groups", "head"), "ctx")

    def whole(queries, *rest):
        body = functools.partial(local, queries.shape[1] // HEAD_DIM)
        return jax.shard_map(
            body, mesh=mesh, in_specs=in_specs, out_specs=out_specs, check_vma=False)(queries, *rest)
    return whole
```
